32 devices in a mesh: dp: 8 (over z, core), tp: 4 (over y, x).
Axes of the slice: x: 2, y: 2, z: 4, core: 2. Of those that a mesh axis runs over, the one named last changes fastest.
Arguments:
- inputs: bfloat16 [8, 4, 1024, 1152], P('dp', None, 'tp'), may hold values from -6 to 6
- cotangent: bfloat16 [8, 4, 1024, 1152], P('dp', None, 'tp'), may hold values from -6 to 6
- bucket_ids: int32 [8], P('dp'), may hold values from 0 to 2, as said below
- patch_mask: int32 [8, 1024], P('dp'), may hold values 0 or 1
- caption: bfloat16 [8, 120, 4096], P('dp'), may hold values from -6 to 6
- caption_mask: int32 [8, 120], P('dp'), may hold values from 0 to 1, as said below
- conditioning: float32 [8, 6, 1152], P('dp'), may hold values from -2 to 2
- mod_table: float32 [2, 6, 1152], replicated, may hold values from -2 to 2
- spatial_qkv: bfloat16 [1152, 3, 1152], P(None, None, 'tp'), may hold values from -0.1875 to 0.1875
- spatial_out: bfloat16 [1152, 1152], P('tp'), may hold values from -1 to 1
- spatial_up: bfloat16 [1152, 4608], P(None, 'tp'), may hold values from -0.1875 to 0.1875
- spatial_down: bfloat16 [4608, 1152], P('tp'), may hold values from -0.09375 to 0.09375
- temporal_qkv: bfloat16 [1152, 3, 1152], P(None, None, 'tp'), may hold values from -0.1875 to 0.1875
- temporal_out: bfloat16 [1152, 1152], P('tp'), may hold values from -0.25 to 0.25
- cross_query: bfloat16 [1152, 1152], P(None, 'tp'), may hold values from -0.1875 to 0.1875
- cross_kv: bfloat16 [4096, 2, 1152], P(None, None, 'tp'), may hold values from -0.09375 to 0.09375
- cross_out: bfloat16 [1152, 1152], P('tp'), may hold values from -0.5 to 0.5
- temporal_up: bfloat16 [1152, 4608], P(None, 'tp'), may hold values from -0.1875 to 0.1875
- temporal_down: bfloat16 [4608, 1152], P('tp'), may hold values from -0.09375 to 0.09375
Outputs:
- output: bfloat16 [8, 4, 1024, 1152], P('dp', None, 'tp')
- input_grad: bfloat16 [8, 4, 1024, 1152], P('dp', None, 'tp')
- mod_table_grad: float32 [2, 6, 1152], P(None, None, ('dp', 'tp'))
- spatial_qkv_grad: float32 [1152, 3, 1152], P('dp', None, 'tp')
- spatial_out_grad: float32 [1152, 1152], P('tp', 'dp')
- spatial_up_grad: float32 [1152, 4608], P('dp', 'tp')
- spatial_down_grad: float32 [4608, 1152], P('tp', 'dp')
- temporal_qkv_grad: float32 [1152, 3, 1152], P('dp', None, 'tp')
- temporal_out_grad: float32 [1152, 1152], P('tp', 'dp')
- cross_query_grad: float32 [1152, 1152], P('dp', 'tp')
- cross_kv_grad: float32 [4096, 2, 1152], P('dp', None, 'tp')
- cross_out_grad: float32 [1152, 1152], P('tp', 'dp')
- temporal_up_grad: float32 [1152, 4608], P('dp', 'tp')
- temporal_down_grad: float32 [4608, 1152], P('tp', 'dp')
The draws below stay inside these ranges and needn't reach their ends.
Inputs may be any that keep to these rules, and one draw needn't show every extreme that they name: `bucket_ids`: bucket b gives a clip the first 1024 - b * (256) patch positions of each frame; every bucket occurs. `caption_mask`: in each clip the ones form a prefix of 15 or more positions, and every clip has some zeros.
All inputs are finite; a program needn't handle non-finite values. No bound on the sum of `patch_mask` on one device may be relied on, other than what follows from the above.
Results may differ from the reference program's by a relative error of at most 0.03.
Values may be sent and summed in bfloat16 or wider, within the bound.
No kernel may reach another device: no remote copies, remote signals or barrier semaphores. Data moves between devices by JAX's collectives and lax.ppermute only.
A program may use at most 448 MiB of HBM per device.

```python
import jax
import jax.numpy as jnp
from jax import lax

D = 1152
HEADS = 16
HEAD_DIM = 72
FF = 4608
CAP_D = 4096
CAP_LEN = 120
PATCHES = 1024
FRAMES = 4
CLIPS = 8


def draw_bucket_ids(key, part):
    key = jax.random.fold_in(key, 11)
    shuffled = jax.random.permutation(key, CLIPS)
    return (shuffled % 3).astype(jnp.int32)


def draw_caption_mask(key, part):
    key = jax.random.fold_in(key, 12)
    counts = jax.random.randint(key, (CLIPS,), CAP_LEN // 8, CAP_LEN)
    places = jnp.arange(CAP_LEN)
    return (places[None, :] < counts[:, None]).astype(jnp.int32)


def plant(array, key, smallest, largest):
    shape = array.shape
    spot = [jax.random.randint(jax.random.fold_in(key, axis), (), 0, shape[axis]) for axis in range(len(shape))]
    array = array.at[tuple(spot)].set(smallest)
    longest = shape.index(max(shape))
    spot[longest] = (spot[longest] + 1) % shape[longest]
    return array.at[tuple(spot)].set(largest)


def levels(rng, extent, pieces, smallest, top_value):
    loudness = 1.0
    for dim, blocks in pieces:
        draws = jax.random.uniform(jax.random.fold_in(jax.random.fold_in(rng, 6), dim), (blocks,), jnp.float32, smallest / len(pieces), top_value / len(pieces))
        loudness = loudness * jnp.repeat(jnp.exp(draws), extent[dim] // blocks).reshape((-1,) + (1,) * (len(extent) - 1 - dim))
    return loudness


def gaussian(rng, dims, scale, limit, split=(), kind=jnp.bfloat16):
    loudness = levels(rng, dims, split, -0.22, 0.18) if split else 1.0
    values = jax.random.normal(rng, dims, jnp.float32) * scale * loudness
    return jnp.minimum(jnp.maximum(values, -limit), limit).astype(kind)


def setup_inputs(seed: int = 0) -> dict:
    key_of = jax.random.split(jax.random.key(seed), 20)
    inputs = gaussian(key_of[0], (CLIPS, FRAMES, PATCHES, D), 1.0, 6.0, ((0, 8), (2, 4)))
    cotangent = gaussian(key_of[1], (CLIPS, FRAMES, PATCHES, D), 1.0, 6.0, ((0, 8), (2, 4)))
    bucket_ids = draw_bucket_ids(jax.random.fold_in(key_of[19], 71), 0)
    patch_mask = plant((jax.random.randint(key_of[3], (CLIPS, PATCHES), 0, 8) < 7).astype(jnp.int32), jax.random.fold_in(key_of[3], 1), 0, 1)
    caption = gaussian(key_of[4], (CLIPS, CAP_LEN, CAP_D), 1.0, 6.0, ((0, 8),))
    caption_mask = draw_caption_mask(jax.random.fold_in(key_of[19], 71), 0)
    conditioning = gaussian(key_of[6], (CLIPS, 6, D), 0.25, 2.0, ((0, 8),), jnp.float32)
    mod_table = gaussian(key_of[7], (2, 6, D), 0.25, 2.0, (), jnp.float32)
    spatial_qkv = gaussian(key_of[8], (D, 3, HEADS * HEAD_DIM), D ** -0.5, 0.1875, ((2, 4),))
    spatial_out = gaussian(key_of[9], (HEADS * HEAD_DIM, D), (D // 32) ** -0.5, 1.0, ((0, 4),))
    spatial_up = gaussian(key_of[10], (D, FF), D ** -0.5, 0.1875, ((1, 4),))
    spatial_down = gaussian(key_of[11], (FF, D), FF ** -0.5, 0.09375, ((0, 4),))
    temporal_qkv = gaussian(key_of[12], (D, 3, HEADS * HEAD_DIM), D ** -0.5, 0.1875, ((2, 4),))
    temporal_out = gaussian(key_of[13], (HEADS * HEAD_DIM, D), (D // 2) ** -0.5, 0.25, ((0, 4),))
    cross_query = gaussian(key_of[14], (D, HEADS * HEAD_DIM), D ** -0.5, 0.1875, ((1, 4),))
    cross_kv = gaussian(key_of[15], (CAP_D, 2, HEADS * HEAD_DIM), CAP_D ** -0.5, 0.09375, ((2, 4),))
    cross_out = gaussian(key_of[16], (HEADS * HEAD_DIM, D), (D // 8) ** -0.5, 0.5, ((0, 4),))
    temporal_up = gaussian(key_of[17], (D, FF), D ** -0.5, 0.1875, ((1, 4),))
    temporal_down = gaussian(key_of[18], (FF, D), FF ** -0.5, 0.09375, ((0, 4),))
    return dict(inputs=inputs, cotangent=cotangent, bucket_ids=bucket_ids, patch_mask=patch_mask, caption=caption, caption_mask=caption_mask, conditioning=conditioning, mod_table=mod_table, spatial_qkv=spatial_qkv, spatial_out=spatial_out, spatial_up=spatial_up, spatial_down=spatial_down, temporal_qkv=temporal_qkv, temporal_out=temporal_out, cross_query=cross_query, cross_kv=cross_kv, cross_out=cross_out, temporal_up=temporal_up, temporal_down=temporal_down)


epsilon = 1e-06
masked_score = -1e+30

@jax.custom_vjp
def low(v):
    return lax.optimization_barrier(v.astype(jnp.bfloat16)).astype(jnp.float32)

@jax.custom_vjp
def low_back(v):
    return v

def low_keep(v):
    return (low(v), None)

def low_pass(kept, grad):
    return (grad,)

def back_keep(v):
    return (v, None)

def back_low(kept, grad):
    return (low(grad),)
low.defvjp(low_keep, low_pass)
low_back.defvjp(back_keep, back_low)

def round_both(values_in):
    return low_back(low(values_in))

def product(form, left, right):
    return jnp.einsum(form, left, right, precision=lax.Precision.HIGHEST)

def norm_mod(values_in, shifting, scaling):
    centre = values_in - lax.optimization_barrier(jnp.mean(values_in, axis=-1, keepdims=True))
    spread = lax.optimization_barrier(jnp.mean(centre * centre, axis=-1, keepdims=True))
    return centre * lax.rsqrt(spread + epsilon) * (1.0 + scaling) + shifting

def gelu_tanh(values_in):
    return jax.nn.gelu(values_in, approximate=True)

def attend(query_rows, key_rows, value_rows, keep_mask):
    scaling = query_rows.shape[-1] ** (-0.5)
    scores = low_back(product('bqhe,bkhe->bhqk', query_rows, key_rows) * scaling)
    scores = jnp.where(keep_mask[:, None, None, :], scores, masked_score)
    weights = low(jax.nn.softmax(scores, axis=-1))
    return round_both(product('bhqk,bkhe->bqhe', weights, value_rows))

def self_attention(resid, modulation, qkv_weight, out_weight, runner):
    normed = low(norm_mod(resid, modulation[0], modulation[1]))
    projected = round_both(product('fpd,dkc->fpkc', normed, qkv_weight))
    head_rows = [projected[:, :, column].reshape(FRAMES, PATCHES, HEADS, HEAD_DIM) for column in range(3)]
    mixed_heads = runner(head_rows[0], head_rows[1], head_rows[2]).reshape(FRAMES, PATCHES, HEADS * HEAD_DIM)
    branch = low_back(product('fpc,cd->fpd', mixed_heads, out_weight))
    return resid + modulation[2] * branch

def feed_forward(resid, modulation, up_weight, down_weight):
    normed = low(norm_mod(resid, modulation[3], modulation[4]))
    upward = low_back(product('fpd,dc->fpc', normed, up_weight))
    hidden = low(gelu_tanh(upward))
    branch = low_back(product('fpc,cd->fpd', hidden, down_weight))
    return resid + modulation[5] * branch

def clip_forward(resid, weights, cond_row, caption_rows, caption_keep, valid_row):
    table_rows, spatial_qkv, spatial_out, spatial_up, spatial_down, temporal_qkv, temporal_out, cross_query, cross_kv, cross_out, temporal_up, temporal_down = weights
    first_mod = table_rows[0] + cond_row
    second_mod = table_rows[1] + cond_row
    frame_keep = jnp.broadcast_to(valid_row, (FRAMES, PATCHES))

    def spatial_runner(query_rows, key_rows, value_rows):

        def one_frame(frame_item):
            return attend(*(member[None] for member in frame_item))[0]
        return lax.map(jax.checkpoint(one_frame), (query_rows, key_rows, value_rows, frame_keep))

    def temporal_runner(query_rows, key_rows, value_rows):
        keep_all = jnp.ones((PATCHES, FRAMES), dtype=jnp.bool_)
        swapped = [jnp.swapaxes(member, 0, 1) for member in (query_rows, key_rows, value_rows)]
        return jnp.swapaxes(attend(swapped[0], swapped[1], swapped[2], keep_all), 0, 1)
    resid = self_attention(resid, first_mod, spatial_qkv, spatial_out, spatial_runner)
    cross_in = low(resid)
    cross_rows = round_both(product('fpd,dc->fpc', cross_in, cross_query)).reshape(1, FRAMES * PATCHES, HEADS, HEAD_DIM)
    caption_kv = round_both(product('ld,dkc->lkc', caption_rows, cross_kv))
    caption_key = caption_kv[:, 0].reshape(1, CAP_LEN, HEADS, HEAD_DIM)
    caption_value = caption_kv[:, 1].reshape(1, CAP_LEN, HEADS, HEAD_DIM)
    mixed_heads = attend(cross_rows, caption_key, caption_value, caption_keep[None]).reshape(FRAMES, PATCHES, HEADS * HEAD_DIM)
    resid = resid + low_back(product('fpc,cd->fpd', mixed_heads, cross_out))
    resid = feed_forward(resid, first_mod, spatial_up, spatial_down)
    resid = self_attention(resid, second_mod, temporal_qkv, temporal_out, temporal_runner)
    resid = feed_forward(resid, second_mod, temporal_up, temporal_down)
    return valid_row.astype(jnp.float32)[None, :, None] * resid

def reference(inputs, cotangent, bucket_ids, patch_mask, caption, caption_mask, conditioning, mod_table, spatial_qkv, spatial_out, spatial_up, spatial_down, temporal_qkv, temporal_out, cross_query, cross_kv, cross_out, temporal_up, temporal_down):
    weights = tuple((matrix.astype(jnp.float32) for matrix in (mod_table, spatial_qkv, spatial_out, spatial_up, spatial_down, temporal_qkv, temporal_out, cross_query, cross_kv, cross_out, temporal_up, temporal_down)))
    patch_count = PATCHES - bucket_ids * (PATCHES // 4)
    valid_mask = (jnp.arange(PATCHES)[None, :] < patch_count[:, None]) & (patch_mask == 1)

    def one_clip(summed, clip_item):
        clip_in, clip_cot, clip_caption, clip_keep, clip_cond, clip_valid = clip_item

        def forward(resid, params):
            return clip_forward(resid, params, clip_cond, clip_caption, clip_keep, clip_valid)
        result, pullback = jax.vjp(forward, clip_in.astype(jnp.float32), weights)
        grad_in, grad_params = pullback(clip_cot.astype(jnp.float32))
        summed = jax.tree.map(lambda left, right: left + right, summed, grad_params)
        return (summed, (result.astype(jnp.bfloat16), grad_in.astype(jnp.bfloat16)))
    zero_grads = jax.tree.map(jnp.zeros_like, weights)
    summed, (output, input_grad) = lax.scan(one_clip, zero_grads, (inputs, cotangent, caption.astype(jnp.float32), caption_mask == 1, conditioning, valid_mask))
    return (output, input_grad, summed[0], summed[1], summed[2], summed[3], summed[4], summed[5], summed[6], summed[7], summed[8], summed[9], summed[10], summed[11])
```

```python
import functools

import jax
import jax.numpy as jnp
from jax import lax
from jax.experimental import pallas as pl
from jax.experimental.pallas import tpu as pltpu
from jax.sharding import PartitionSpec as P

HEAD_DIM = 72
LOG2E = 1.4426950408889634
LN2 = 0.6931471805599453
EPSILON = 1e-06
MASKED = -1e30
F32 = jnp.float32
BF16 = jnp.bfloat16
VMEM_LIMIT = 56 * 2**20


def dot(left, right, left_dim, right_dim):
    return lax.dot_general(
        left, right, (((left_dim,), (right_dim,)), ((), ())), preferred_element_type=F32
    )


def attend_kernel(block, q_ref, k_ref, v_ref, bias_ref, o_ref, total_ref):
    keys, values, bias = k_ref[0], v_ref[0], bias_ref[...]
    for first in range(0, q_ref.shape[2], block):
        part = slice(first, first + block)
        scores = dot(keys, q_ref[0, :, part], 0, 0) + bias
        top = jnp.max(scores, axis=0, keepdims=True)
        weights = jnp.exp2(scores - top)
        total = jnp.sum(weights, axis=0, keepdims=True)
        outcome = dot(values, weights.astype(BF16), 1, 0)
        o_ref[0, :, part] = (outcome / total).astype(BF16)
        total_ref[0, :, part] = top + jnp.log2(total)


def attend_back_kernel(
    block, q_ref, k_ref, v_ref, bias_ref, o_ref, total_ref, do_ref, dq_ref, dk_ref, dv_ref
):
    keys, values, bias = k_ref[0], v_ref[0], bias_ref[...]
    grad_keys = jnp.zeros(keys.shape, F32)
    grad_values = jnp.zeros(values.shape, F32)
    for first in range(0, q_ref.shape[2], block):
        part = slice(first, first + block)
        query, grad = q_ref[0, :, part], do_ref[0, :, part]
        weighted = jnp.sum(
            grad.astype(F32) * o_ref[0, :, part].astype(F32), axis=0, keepdims=True
        )
        scores = dot(keys, query, 0, 0) + bias
        probs = jnp.exp2(scores - total_ref[0, :, part])
        grad_probs = dot(values, grad, 0, 0)
        grad_scores = (probs * (grad_probs - weighted)).astype(BF16)
        dq_ref[0, :, part] = (dot(keys, grad_scores, 1, 0) * HEAD_DIM**-0.5).astype(BF16)
        grad_keys = grad_keys + dot(query, grad_scores, 1, 1)
        grad_values = grad_values + dot(grad, probs.astype(BF16), 1, 1)
    dk_ref[0] = (grad_keys * LN2).astype(BF16)
    dv_ref[0] = grad_values.astype(BF16)


def head_spec(width, rows=HEAD_DIM):
    return pl.BlockSpec((1, rows, width), lambda head: (head, 0, 0))


def attend(query, keys, values, bias):
    heads, _, queries = query.shape
    length = keys.shape[2]
    return pl.pallas_call(
        functools.partial(attend_kernel, min(512, queries)),
        grid=(heads,),
        in_specs=[
            head_spec(queries),
            head_spec(length),
            head_spec(length),
            pl.BlockSpec((length, 1), lambda head: (0, 0)),
        ],
        out_specs=[head_spec(queries), head_spec(queries, 1)],
        out_shape=[
            jax.ShapeDtypeStruct(query.shape, BF16),
            jax.ShapeDtypeStruct((heads, 1, queries), F32),
        ],
        compiler_params=pltpu.CompilerParams(vmem_limit_bytes=VMEM_LIMIT),
        cost_estimate=pl.CostEstimate(
            flops=heads * queries * length * 1024,
            bytes_accessed=query.size * 8,
            transcendentals=heads * queries * length,
        ),
    )(query, keys, values, bias)


def attend_back(query, keys, values, bias, outcome, total, grad):
    heads, _, queries = query.shape
    length = keys.shape[2]
    return pl.pallas_call(
        functools.partial(attend_back_kernel, min(512, queries)),
        grid=(heads,),
        in_specs=[
            head_spec(queries),
            head_spec(length),
            head_spec(length),
            pl.BlockSpec((length, 1), lambda head: (0, 0)),
            head_spec(queries),
            head_spec(queries, 1),
            head_spec(queries),
        ],
        out_specs=[head_spec(queries), head_spec(length), head_spec(length)],
        out_shape=[
            jax.ShapeDtypeStruct(query.shape, BF16),
            jax.ShapeDtypeStruct(keys.shape, BF16),
            jax.ShapeDtypeStruct(keys.shape, BF16),
        ],
        compiler_params=pltpu.CompilerParams(vmem_limit_bytes=VMEM_LIMIT),
        cost_estimate=pl.CostEstimate(
            flops=heads * queries * length * 2560,
            bytes_accessed=query.size * 16,
            transcendentals=heads * queries * length,
        ),
    )(query, keys, values, bias, outcome, total, grad)


def frame_columns(ref, frames):
    width = ref.shape[2] // frames
    return [ref[0, :, f * width : (f + 1) * width].astype(F32) for f in range(frames)]


def column_sum(left, right):
    return jnp.sum(left * right, axis=0, keepdims=True)


def frame_probs(query, keys):
    result = []
    for one in query:
        scores = [column_sum(one, other) for other in keys]
        top = functools.reduce(jnp.maximum, scores)
        weights = [jnp.exp2(score - top) for score in scores]
        inverse = 1.0 / functools.reduce(jnp.add, weights)
        result.append([weight * inverse for weight in weights])
    return result


def rounded(value):
    return value.astype(BF16).astype(F32)


def store_frames(ref, columns, scale=None):
    width = columns[0].shape[1]
    for f, column in enumerate(columns):
        column = column if scale is None else column * scale
        ref[0, :, f * width : (f + 1) * width] = column.astype(BF16)


def mix(weights, columns):
    return functools.reduce(jnp.add, [w * column for w, column in zip(weights, columns)])


def across_kernel(frames, q_ref, k_ref, v_ref, o_ref):
    query, keys, values = [frame_columns(ref, frames) for ref in (q_ref, k_ref, v_ref)]
    probs = frame_probs(query, keys)
    store_frames(o_ref, [mix([rounded(p) for p in row], values) for row in probs])


def across_back_kernel(frames, q_ref, k_ref, v_ref, do_ref, dq_ref, dk_ref, dv_ref):
    query, keys, values, grad = [
        frame_columns(ref, frames) for ref in (q_ref, k_ref, v_ref, do_ref)
    ]
    probs = frame_probs(query, keys)
    grad_scores = []
    for f in range(frames):
        grad_probs = [column_sum(grad[f], value) for value in values]
        weighted = mix(probs[f], grad_probs)
        grad_scores.append(
            [rounded(p * (gp - weighted)) for p, gp in zip(probs[f], grad_probs)]
        )
    store_frames(dq_ref, [mix(row, keys) for row in grad_scores], HEAD_DIM**-0.5)
    turned = list(zip(*grad_scores))
    store_frames(dk_ref, [mix(column, query) for column in turned], LN2)
    turned = [[rounded(p) for p in column] for column in zip(*probs)]
    store_frames(dv_ref, [mix(column, grad) for column in turned])


def across(kernel, frames, operands, results):
    heads, _, tokens = operands[0].shape
    shape = jax.ShapeDtypeStruct(operands[0].shape, BF16)
    return pl.pallas_call(
        functools.partial(kernel, frames),
        grid=(heads,),
        in_specs=[head_spec(tokens)] * len(operands),
        out_specs=[head_spec(tokens)] * results,
        out_shape=[shape] * results,
        compiler_params=pltpu.CompilerParams(vmem_limit_bytes=VMEM_LIMIT),
        cost_estimate=pl.CostEstimate(
            flops=operands[0].size * 64,
            bytes_accessed=operands[0].size * 8,
            transcendentals=heads * tokens * frames,
        ),
    )(*operands)


def norm_parts(resid):
    centre = resid - jnp.mean(resid, axis=-1, keepdims=True)
    inverse = lax.rsqrt(jnp.mean(centre * centre, axis=-1, keepdims=True) + EPSILON)
    return centre * inverse, inverse


def norm_rows(resid, shift, scale):
    return (norm_parts(resid)[0] * (1.0 + scale) + shift).astype(BF16)


def norm_back(resid, scale, grad):
    normal, inverse = norm_parts(resid)
    grad_normal = grad * (1.0 + scale)
    change = (
        grad_normal
        - jnp.mean(grad_normal, axis=-1, keepdims=True)
        - normal * jnp.mean(grad_normal * normal, axis=-1, keepdims=True)
    ) * inverse
    return change, jnp.sum(grad, axis=0), jnp.sum(grad * normal, axis=0)


def gelu_parts(value):
    factor = 0.7978845608028654
    square = value * value
    bend = jnp.tanh(factor * value * (1.0 + 0.044715 * square))
    half = 0.5 * (1.0 + bend)
    slope = half + 0.5 * value * (1.0 - bend * bend) * factor * (1.0 + 0.134145 * square)
    return value * half, slope


def on_device(
    mesh_shape,
    inputs,
    cotangent,
    bucket_ids,
    patch_mask,
    caption,
    caption_mask,
    conditioning,
    mod_table,
    spatial_qkv,
    spatial_out,
    spatial_up,
    spatial_down,
    temporal_qkv,
    temporal_out,
    cross_query,
    cross_kv,
    cross_out,
    temporal_up,
    temporal_down,
):
    tp, dp = mesh_shape["tp"], mesh_shape["dp"]
    _, frames, local_patches, features = inputs.shape
    patches = patch_mask.shape[1]
    parts = tp // frames
    here = lax.axis_index("tp")
    core = lax.axis_index("dp") % 2
    tokens = frames * local_patches

    def swap_tp(value, step):
        return lax.ppermute(value, "tp", [(i, i ^ step) for i in range(tp)])

    def swap_core(value):
        return lax.ppermute(value, "dp", [(i, i ^ 1) for i in range(dp)])

    def after(value, earlier):
        return lax.optimization_barrier((value, earlier))[0]

    def exchange(chunks):
        return [chunks[0]] + [swap_tp(chunks[k], k) for k in range(1, frames)]

    def gather_tp(block, gate=None):
        if gate is not None:
            block = after(block, gate)
        if tp != 4:
            held = [block]
            for bit in (1 << b for b in range(tp.bit_length() - 1)):
                held = held + [swap_tp(piece, bit) for piece in held]
            return [[piece] for piece in held], held[1]
        half = block.shape[0] // 2
        from_x, from_y = swap_tp(block, 1), swap_tp(block, 2)
        top, bottom = swap_tp(from_y[:half], 1), swap_tp(from_x[half:], 2)
        return [[block], [from_x], [from_y], [top, bottom]], (from_x, from_y)

    def scatter_tp(blocks):
        def reduce(held, bits):
            for bit in bits:
                sent = [k for k in held if k & bit]
                arrived = {k ^ bit: swap_tp(held[k], bit) for k in sent}
                held = {k: held[k] + arrived[k] for k in arrived}
            return held[0]

        bits = [1 << b for b in range(tp.bit_length() - 1)]
        half = blocks[0].shape[0] // 2
        return jnp.concatenate(
            [
                reduce({k: block[:half] for k, block in enumerate(blocks)}, bits),
                reduce({k: block[half:] for k, block in enumerate(blocks)}, bits[::-1]),
            ],
            axis=0,
        )

    def rows_of(weight):
        turned = jnp.moveaxis(weight, 0, -1)
        return turned if turned.ndim == 3 else turned[None]

    def halves_of(weight):
        kinds, rows, _ = weight.shape
        halved = weight.reshape(kinds, 2, rows // 2, features)
        own = lax.dynamic_index_in_dim(halved, core, 1, keepdims=False)
        other = lax.dynamic_index_in_dim(halved, 1 - core, 1, keepdims=False)
        return own.reshape(-1, features), other.reshape(-1, features)

    groups = [
        [rows_of(spatial_qkv)],
        [spatial_out[None], rows_of(cross_query), cross_out[None]],
        [rows_of(spatial_up)],
        [spatial_down[None]],
        [rows_of(temporal_qkv), temporal_out[None]],
        [rows_of(temporal_up)],
        [temporal_down[None]],
    ]

    def gathered(group, gate):
        pairs = [halves_of(weight) for weight in group]
        own = jnp.concatenate([pair[0] for pair in pairs], axis=0)
        other = jnp.concatenate([pair[1] for pair in pairs], axis=0)
        own_blocks, gate = gather_tp(own, gate)
        other_blocks = [[other]] + [[swap_core(p) for p in block] for block in own_blocks[1:]]
        blocks = own_blocks + other_blocks
        result, offset = [], 0
        for weight in group:
            kinds, rows = weight.shape[0], weight.shape[1] // 2
            pieces = []
            for kind in range(kinds):
                low = offset + kind * rows
                for block in blocks:
                    first = 0
                    for piece in block:
                        last = first + piece.shape[0]
                        left, right = max(low, first), min(low + rows, last)
                        if left < right:
                            pieces.append(piece[left - first : right - first])
                        first = last
            result.append(jnp.concatenate(pieces, axis=0))
            offset += kinds * rows
        return result, gate

    def weight_gradient(grad, kinds, minor):
        rows = grad.shape[0] // (kinds * 2 * tp)
        shaped = grad.reshape(kinds, 2, tp, rows, features)
        arrived = swap_core(shaped[:, 1])
        summed = shaped[:, 0] + arrived
        block = scatter_tp([summed[:, k].reshape(kinds * rows, features) for k in range(tp)])
        column = lax.psum_scatter(
            block,
            "dp",
            scatter_dimension=1,
            tiled=True,
            axis_index_groups=[list(range(c, dp, 2)) for c in range(2)],
        )
        width = features // dp
        column = column.reshape(kinds, rows, 2, width)
        kept = lax.dynamic_index_in_dim(column, core, 2, keepdims=False)
        sent = lax.dynamic_index_in_dim(column, 1 - core, 2, keepdims=False)
        pair = [kept, swap_core(sent)]
        both = jnp.where(core == 0, jnp.stack(pair, 1), jnp.stack(pair[::-1], 1))
        both = both.reshape(kinds, 2 * rows, width).astype(F32)
        if minor:
            return both[0]
        turned = jnp.moveaxis(both, 2, 0)
        return turned if kinds > 1 else turned[:, 0]

    patch_count = patches - bucket_ids[0] * (patches // 4)
    valid = (jnp.arange(patches) < patch_count) & (patch_mask[0] == 1)
    valid_blocks = valid.reshape(tp, local_patches)

    def valid_at(index):
        return lax.dynamic_index_in_dim(valid_blocks, index, 0, keepdims=False)

    first_mates = [
        [part * frames + ((here % frames) ^ k) for k in range(frames)] for part in range(parts)
    ]
    frame_valid = jnp.concatenate([valid_at(mate) for row in first_mates for mate in row])
    frame_bias = jnp.where(frame_valid, 0.0, MASKED).astype(F32)[:, None]
    valid_local = jnp.tile(valid_at(here).astype(F32), frames)[:, None]
    caption_length = caption.shape[1]
    caption_room = -(-caption_length // 128) * 128
    caption_keep = jnp.pad(caption_mask[0], (0, caption_room - caption_length)) == 1
    caption_bias = jnp.where(caption_keep, 0.0, MASKED).astype(F32)[:, None]
    modulation = mod_table + conditioning

    def frame_index(k):
        return (here % frames) ^ k

    def by_neighbour(value):
        return [
            lax.dynamic_index_in_dim(value, frame_index(k), 0, keepdims=False)
            for k in range(frames)
        ]

    def relayout(value):
        chunks = value.reshape(frames, local_patches, features)
        return jnp.concatenate(exchange([chunks[k] for k in range(frames)]), axis=0)

    def heads_of(value):
        return value.reshape(-1, HEAD_DIM, value.shape[-1])

    def flat(value):
        return value.reshape(-1, value.shape[-1])

    mates = [[f + frames * part for part in range(parts)] for f in range(frames)]

    def all_keys(value):
        if parts == 1:
            return value
        return lax.all_gather(value, "tp", axis=2, tiled=True, axis_index_groups=mates)

    def own_keys(value):
        if parts == 1:
            return value
        return lax.psum_scatter(
            value, "tp", scatter_dimension=2, tiled=True, axis_index_groups=mates
        )

    scaled = HEAD_DIM**-0.5 * LOG2E

    def project(weight, rows):
        return jnp.einsum("rd,td->rt", weight, rows, preferred_element_type=F32)

    def qkv_of(weight, rows):
        projected = project(weight, rows)
        width = projected.shape[0] // 3
        query = (projected[:width] * scaled).astype(BF16)
        keys = projected[width : 2 * width].astype(BF16)
        values = projected[2 * width :].astype(BF16)
        return heads_of(query), heads_of(keys), heads_of(values)

    def unproject(columns, weight):
        return jnp.einsum("ft,fd->td", columns, weight, preferred_element_type=F32)

    def outer(columns, rows):
        return jnp.einsum(
            "ft,td->fd", columns, rows, preferred_element_type=F32
        ).astype(BF16)

    chunks = by_neighbour(inputs[0])
    resid_zero = jnp.concatenate(exchange(chunks), axis=0).astype(F32)

    (space_qkv,), gate = gathered(groups[0], None)
    (space_out, cross_q, cross_o), gate = gathered(groups[1], gate)
    (space_up,), gate = gathered(groups[2], gate)
    (space_down,), gate = gathered(groups[3], gate)
    (time_qkv, time_out), gate = gathered(groups[4], gate)
    (time_up,), gate = gathered(groups[5], gate)
    (time_down,), gate = gathered(groups[6], gate)

    caption_kv = jnp.einsum(
        "dkx,ld->kxl", cross_kv, caption[0], preferred_element_type=F32
    ).astype(BF16)
    caption_kv = jnp.pad(caption_kv, ((0, 0), (0, 0), (0, caption_room - caption_length)))
    heads_local = caption_kv.shape[1]
    kv_blocks, _ = gather_tp(caption_kv.reshape(2 * heads_local, caption_room))
    kv_blocks = [jnp.concatenate(block, axis=0) for block in kv_blocks]
    kv_all = jnp.stack(kv_blocks).reshape(tp, 2, 2, heads_local // 2, caption_room)
    kv_all = jnp.concatenate(
        [
            lax.dynamic_index_in_dim(kv_all, core, 2, keepdims=False),
            lax.dynamic_index_in_dim(kv_all, 1 - core, 2, keepdims=False),
        ],
        axis=0,
    )
    caption_keys = heads_of(flat(kv_all[:, 0]))
    caption_values = heads_of(flat(kv_all[:, 1]))
    caption_all = lax.all_gather(caption, "dp", axis=0, tiled=True)

    row = lambda layer, column: modulation[layer, column]
    rows_a = norm_rows(resid_zero, row(0, 0), row(0, 1))
    query_a, keys_a, values_a = qkv_of(space_qkv, rows_a)
    keys_a, values_a = all_keys(keys_a), all_keys(values_a)
    mixed_a, total_a = attend(query_a, keys_a, values_a, frame_bias)
    branch_a = unproject(flat(mixed_a), space_out)
    resid_one = resid_zero + row(0, 2) * branch_a

    rows_c = resid_one.astype(BF16)
    query_c = heads_of((project(cross_q, rows_c) * scaled).astype(BF16))
    mixed_c, total_c = attend(query_c, caption_keys, caption_values, caption_bias)
    resid_two = resid_one + unproject(flat(mixed_c), cross_o)

    def mlp_forward(resid, layer, up, down):
        rows = norm_rows(resid, row(layer, 3), row(layer, 4))
        hidden, slope = gelu_parts(project(up, rows))
        hidden, slope = hidden.astype(BF16), slope.astype(BF16)
        branch = unproject(hidden, down)
        return resid + row(layer, 5) * branch, (resid, rows, hidden, slope, branch)

    resid_three, kept_a = mlp_forward(resid_two, 0, space_up, space_down)

    resid_three = relayout(resid_three.astype(BF16)).astype(F32)
    rows_t = norm_rows(resid_three, row(1, 0), row(1, 1))
    query_t, keys_t, values_t = qkv_of(time_qkv, rows_t)
    (mixed_t,) = across(across_kernel, frames, (query_t, keys_t, values_t), 1)
    branch_t = unproject(flat(mixed_t), time_out)
    resid_four = resid_three + row(1, 2) * branch_t
    resid_five, kept_t = mlp_forward(resid_four, 1, time_up, time_down)

    def in_order(value):
        return jnp.concatenate(by_neighbour(value.reshape(frames, local_patches, features)), axis=0)

    output = in_order((valid_local * resid_five).astype(BF16)).reshape(inputs.shape)

    def mlp_backward(grad, layer, up, down, kept):
        resid, rows, hidden, slope, branch = kept
        grad_gate = jnp.sum(grad * branch, axis=0)
        grad_branch = (row(layer, 5) * grad).astype(BF16)
        grad_hidden = project(down, grad_branch)
        grad_up = (grad_hidden * slope.astype(F32)).astype(BF16)
        grad_down_weight = outer(hidden, grad_branch)
        grad_up_weight = outer(grad_up, rows)
        change, grad_shift, grad_scale = norm_back(
            resid, row(layer, 4), unproject(grad_up, up)
        )
        return grad + change, (grad_shift, grad_scale, grad_gate), grad_up_weight, grad_down_weight

    def attention_backward(grad, layer, qkv, out, resid, rows, mixed, branch, run):
        grad_gate = jnp.sum(grad * branch, axis=0)
        grad_branch = (row(layer, 2) * grad).astype(BF16)
        grad_out_weight = outer(flat(mixed), grad_branch)
        grad_mixed = heads_of(project(out, grad_branch).astype(BF16))
        grad_all = jnp.concatenate([flat(member) for member in run(grad_mixed)], axis=0)
        grad_qkv_weight = outer(grad_all, rows)
        change, grad_shift, grad_scale = norm_back(
            resid, row(layer, 1), unproject(grad_all, qkv)
        )
        return grad + change, (grad_shift, grad_scale, grad_gate), grad_qkv_weight, grad_out_weight

    gradient = in_order(cotangent[0]).astype(F32) * valid_local
    gradient, mods_tm, grad_time_up, grad_time_down = mlp_backward(
        gradient, 1, time_up, time_down, kept_t
    )
    grad_time_down = weight_gradient(grad_time_down, 1, True)
    grad_time_up = weight_gradient(grad_time_up, 1, False)

    def run_time(grad_mixed):
        return across(across_back_kernel, frames, (query_t, keys_t, values_t, grad_mixed), 3)

    gradient, mods_ta, grad_time_qkv, grad_time_out = attention_backward(
        gradient, 1, time_qkv, time_out, resid_three, rows_t, mixed_t, branch_t, run_time
    )
    grad_time_out = weight_gradient(grad_time_out, 1, True)
    grad_time_qkv = weight_gradient(grad_time_qkv, 3, False)

    gradient = relayout(gradient.astype(BF16)).astype(F32)
    gradient, mods_sm, grad_space_up, grad_space_down = mlp_backward(
        gradient, 0, space_up, space_down, kept_a
    )
    grad_space_down = weight_gradient(grad_space_down, 1, True)
    grad_space_up = weight_gradient(grad_space_up, 1, False)

    grad_cross = gradient.astype(BF16)
    grad_cross_out = weight_gradient(outer(flat(mixed_c), grad_cross), 1, True)
    grad_mixed_c = heads_of(project(cross_o, grad_cross).astype(BF16))
    grad_cq, grad_ck, grad_cv = attend_back(
        query_c, caption_keys, caption_values, caption_bias, mixed_c, total_c, grad_mixed_c
    )
    grad_cross_query = weight_gradient(outer(flat(grad_cq), rows_c), 1, False)
    gradient = gradient + unproject(flat(grad_cq), cross_q)

    grad_kv = jnp.stack([flat(grad_ck), flat(grad_cv)])
    grad_kv = grad_kv.reshape(2, 2, tp, heads_local // 2, caption_room)
    pair = [grad_kv[:, 0], grad_kv[:, 1]]
    grad_kv = jnp.where(core == 0, jnp.stack(pair, 2), jnp.stack(pair[::-1], 2))
    grad_kv = jnp.moveaxis(grad_kv, 1, 0).reshape(tp, 2 * heads_local, caption_room)
    grad_kv = scatter_tp([grad_kv[k] for k in range(tp)])
    grad_kv = lax.all_gather(
        grad_kv.reshape(1, 2, heads_local, caption_room)[..., :caption_length],
        "dp",
        axis=0,
        tiled=True,
    )
    kv_rows = cross_kv.shape[0] // dp
    caption_part = lax.dynamic_slice_in_dim(
        caption_all, lax.axis_index("dp") * kv_rows, kv_rows, 2
    )
    grad_cross_kv = jnp.einsum(
        "cld,ckxl->dkx", caption_part, grad_kv, preferred_element_type=F32
    )

    def run_space(grad_mixed):
        grads = attend_back(query_a, keys_a, values_a, frame_bias, mixed_a, total_a, grad_mixed)
        return grads[0], own_keys(grads[1]), own_keys(grads[2])

    gradient, mods_sa, grad_space_qkv, grad_space_out = attention_backward(
        gradient, 0, space_qkv, space_out, resid_zero, rows_a, mixed_a, branch_a, run_space
    )
    grad_space_out = weight_gradient(grad_space_out, 1, True)
    grad_space_qkv = weight_gradient(grad_space_qkv, 3, False)
    input_grad = in_order(relayout(gradient.astype(BF16))).reshape(inputs.shape)

    table = jnp.stack([jnp.stack(mods_sa + mods_sm), jnp.stack(mods_ta + mods_tm)])
    mod_table_grad = lax.psum_scatter(table, ("dp", "tp"), scatter_dimension=2, tiled=True)
    return (
        output,
        input_grad,
        mod_table_grad,
        grad_space_qkv,
        grad_space_out,
        grad_space_up,
        grad_space_down,
        grad_time_qkv,
        grad_time_out,
        grad_cross_query,
        grad_cross_kv,
        grad_cross_out,
        grad_time_up,
        grad_time_down,
    )


def solution(mesh):
    return jax.shard_map(
        functools.partial(on_device, dict(mesh.shape)),
        mesh=mesh,
        in_specs=(
            P("dp", None, "tp", None),
            P("dp", None, "tp", None),
            P("dp"),
            P("dp", None),
            P("dp", None, None),
            P("dp", None),
            P("dp", None, None),
            P(),
            P(None, None, "tp"),
            P("tp", None),
            P(None, "tp"),
            P("tp", None),
            P(None, None, "tp"),
            P("tp", None),
            P(None, "tp"),
            P(None, None, "tp"),
            P("tp", None),
            P(None, "tp"),
            P("tp", None),
        ),
        out_specs=(
            P("dp", None, "tp", None),
            P("dp", None, "tp", None),
            P(None, None, ("dp", "tp")),
            P("dp", None, "tp"),
            P("tp", "dp"),
            P("dp", "tp"),
            P("tp", "dp"),
            P("dp", None, "tp"),
            P("tp", "dp"),
            P("dp", "tp"),
            P("dp", None, "tp"),
            P("tp", "dp"),
            P("dp", "tp"),
            P("tp", "dp"),
        ),
        check_vma=False,
    )
```
